32 devices in a mesh: row: 4 (over z), col: 4 (over y, x), depth: 2 (over core).
Axes of the slice: x: 2, y: 2, z: 4, core: 2. Of those that a mesh axis runs over, the one named last changes fastest.
Arguments:
- a_blocks: bfloat16 [4, 2, 2, 4, 128, 128], P('row', 'depth', None, 'col'), may hold values from -6 to 6
- a_index: int32 [4, 2, 2, 4], P('row', 'depth', None, 'col'), may hold values from 0 to 31, as said below
- a_count: int32 [4, 2, 2], P('row'), may hold values from 1 to 4
- b_blocks: bfloat16 [4, 2, 2, 4, 128, 128], P('col', 'depth', None, 'row'), may hold values from -0.25 to 0.25
- b_index: int32 [4, 2, 2, 4], P('col', 'depth', None, 'row'), may hold values from 0 to 63, as said below
- b_count: int32 [4, 2, 2], P('col'), may hold values from 1 to 4
- c_mask: int32 [16, 32], P('row', ('col', 'depth')), may hold values 0 or 1
Outputs:
- c_matrix: bfloat16 [2048, 4096], P('row', ('col', 'depth'))
The draws below stay inside these ranges and needn't reach their ends.
Inputs may be any that keep to these rules, and one draw needn't show every extreme that they name: `a_index`: within each list the positions of all slots are distinct. `b_index`: within each list the positions of all slots are distinct.
All inputs are finite; a program needn't handle non-finite values. No bound on the sum of `c_mask` on one device may be relied on, other than what follows from the above.
Results may differ from the reference program's by a relative error of at most 0.0049.
Values may be sent and summed in bfloat16 or wider, within the bound.
A program may use at most 64 MiB of HBM per device.

```python
import jax
import jax.numpy as jnp
from jax import lax

BS = 128
PW = 8
STEPS = 2
RB = 4
CB = 8
LA = 4
LB = 4
MB = 16
NB = 32
N_ROW = 4
N_COL = 4
N_DEPTH = 2


def index_lists(key, lists, length, pool):
    keys = jax.random.split(key, lists)
    return jax.vmap(lambda single: jax.random.permutation(single, pool)[:length])(keys).astype(jnp.int32)


def draw_a_index(key, part):
    key = jax.random.fold_in(key, 11)
    flat = index_lists(key, N_ROW * N_DEPTH * STEPS, LA, RB * PW)
    return flat.reshape(N_ROW, N_DEPTH, STEPS, LA)


def draw_b_index(key, part):
    key = jax.random.fold_in(key, 23)
    flat = index_lists(key, N_COL * N_DEPTH * STEPS, LB, PW * CB)
    return flat.reshape(N_COL, N_DEPTH, STEPS, LB)


def draw_a_count(key, part):
    key = jax.random.fold_in(key, 37)
    counts = jax.random.randint(key, (N_ROW, N_DEPTH, STEPS), LA // 4, LA + 1).astype(jnp.int32)
    return counts.at[0, 0, 0].set(LA)


def draw_b_count(key, part):
    key = jax.random.fold_in(key, 41)
    counts = jax.random.randint(key, (N_COL, N_DEPTH, STEPS), LB // 4, LB + 1).astype(jnp.int32)
    return counts.at[0, 0, 0].set(LB)


def plant(drawn, key, smallest, top_value):
    spot = [jax.random.randint(jax.random.fold_in(key, axis), (), 0, length) for axis, length in enumerate(drawn.shape)]
    longest = drawn.shape.index(max(drawn.shape))
    beside = spot[:longest] + [(spot[longest] + 1) % drawn.shape[longest]] + spot[longest + 1:]
    return drawn.at[tuple(spot)].set(smallest).at[tuple(beside)].set(top_value)


def levels(own_key, dims, pieces, smallest, top_value):
    gain = 1.0
    for dim, parts in pieces:
        draws = jax.random.uniform(jax.random.fold_in(jax.random.fold_in(own_key, 6), dim), (parts,), jnp.float32, smallest / len(pieces), top_value / len(pieces))
        gain = gain * jnp.repeat(jnp.exp(draws), dims[dim] // parts).reshape((-1,) + (1,) * (len(dims) - 1 - dim))
    return gain


def scatter_about(rng, shape, deviation, reach, pieces=(), kind=jnp.bfloat16):
    values = jax.random.normal(rng, shape, jnp.float32) * deviation
    if len(pieces) > 0:
        values = levels(rng, shape, pieces, -0.22, 0.18) * values
    return jnp.clip(values, min=-reach, max=reach).astype(kind)


def setup_inputs(seed: int = 0) -> dict:
    streams_of = jax.random.split(jax.random.key(seed), 8)
    return {
        "a_blocks": scatter_about(streams_of[0], (N_ROW, N_DEPTH, STEPS, LA, BS, BS), 1.0, 6.0, ((0, 4), (1, 2), (3, 4))),
        "a_index": draw_a_index(jax.random.fold_in(streams_of[7], 71), 0),
        "a_count": draw_a_count(jax.random.fold_in(streams_of[7], 71), 0),
        "b_blocks": scatter_about(streams_of[3], (N_COL, N_DEPTH, STEPS, LB, BS, BS), (BS * PW * STEPS * N_DEPTH // 8) ** -0.5, 0.25, ((0, 4), (1, 2), (3, 4))),
        "b_index": draw_b_index(jax.random.fold_in(streams_of[7], 71), 0),
        "b_count": draw_b_count(jax.random.fold_in(streams_of[7], 71), 0),
        "c_mask": plant((jax.random.randint(streams_of[6], (MB, NB), 0, 4) < 3).astype(jnp.int32), jax.random.fold_in(streams_of[6], 1), 0, 1),
    }


def panel_term(a_blk, a_idx, a_cnt, b_blk, b_idx, b_cnt):
    f32 = jnp.float32
    live_a = jnp.arange(LA, dtype=jnp.int32) < a_cnt
    onehot_a = ((a_idx[:, None] == jnp.arange(RB * PW, dtype=jnp.int32)[None, :]) & live_a[:, None]).astype(f32)
    dense = jnp.einsum("sp,sxy->pxy", onehot_a, a_blk.astype(f32), precision=lax.Precision.HIGHEST).astype(jnp.bfloat16)
    stacked = dense.reshape(RB, PW, BS, BS).transpose(0, 2, 1, 3).reshape(RB * BS, PW, BS)
    inner_b = b_idx // CB
    column_b = b_idx % CB
    live_b = jnp.arange(LB, dtype=jnp.int32) < b_cnt
    picker = (inner_b[:, None] == jnp.arange(PW, dtype=jnp.int32)[None, :]).astype(f32)
    columns = jnp.einsum("sj,mjk->smk", picker, stacked.astype(f32), precision=lax.Precision.HIGHEST)
    products = jnp.einsum("smk,skl->sml", columns, b_blk.astype(f32), precision=lax.Precision.HIGHEST)
    placer = ((column_b[:, None] == jnp.arange(CB, dtype=jnp.int32)[None, :]) & live_b[:, None]).astype(f32)
    placed = jnp.einsum("sn,sml->mnl", placer, products, precision=lax.Precision.HIGHEST)
    return placed.reshape(RB * BS, CB * BS)


def reference(a_blocks, a_index, a_count, b_blocks, b_index, b_count, c_mask):
    def one_tile(pair):
        grid_row = pair // N_COL
        grid_col = pair % N_COL
        total = jnp.zeros((RB * BS, CB * BS), jnp.float32)
        for group in range(N_DEPTH):
            part = jnp.zeros((RB * BS, CB * BS), jnp.float32)
            for step in range(STEPS):
                part = part + panel_term(a_blocks[grid_row, group, step], a_index[grid_row, group, step],
                                         a_count[grid_row, group, step], b_blocks[grid_col, group, step],
                                         b_index[grid_col, group, step], b_count[grid_col, group, step])
            total = total + lax.optimization_barrier(part.astype(jnp.bfloat16)).astype(jnp.float32)
        kept_mask = lax.dynamic_slice(c_mask, ((grid_row * RB).astype(jnp.int32), (grid_col * CB).astype(jnp.int32)), (RB, CB)).astype(jnp.float32)
        kept = total.reshape(RB, BS, CB, BS) * kept_mask[:, None, :, None]
        return kept.reshape(RB * BS, CB * BS).astype(jnp.bfloat16)

    tiles = lax.map(one_tile, jnp.arange(N_ROW * N_COL, dtype=jnp.int32))
    tiles = tiles.reshape(N_ROW, N_COL, RB * BS, CB * BS).transpose(0, 2, 1, 3)
    return tiles.reshape(N_ROW * RB * BS, N_COL * CB * BS)
```

```python
import functools

import jax
import jax.numpy as jnp
from jax import lax
from jax.experimental import pallas as pl
from jax.experimental.pallas import tpu as pltpu
from jax.sharding import PartitionSpec as P

BS = 128
PW = 8
RB = 4
CB = 8
TAIL = 16
BF = jnp.bfloat16
F32 = jnp.float32


def _rows(values):
    row = lax.broadcasted_iota(jnp.int32, (TAIL, BS), 0)
    tile = jnp.zeros((TAIL, BS), jnp.int32)
    for r, value in enumerate(values):
        tile = jnp.where(row == r, value, tile)
    return tile.astype(F32).astype(BF)


def _times(mask, block):
    return (block.reshape(BS // TAIL, TAIL, BS) * mask[None]).reshape(BS, BS)


def kernel(n_row, n_col, steps,
           a_hbm, ai, ac, b_hbm, bi, bc, cm, out_ref,
           abuf, bbuf, acc,
           load_sem, a_send, a_recv, a_send2, a_recv2,
           b_right, b_left, b_recv, b_send2, b_recv2):
    r = lax.axis_index("row")
    c = lax.axis_index("col")
    d = lax.axis_index("depth")
    sib = {"depth": 1 - d}
    half = CB // 2

    loads = []
    for s in range(steps):
        rows = pl.ds(s * BS, BS)
        loads.append(pltpu.make_async_copy(b_hbm.at[0, 0, s, 0], bbuf.at[0, r, rows], load_sem.at[2 * s]))
        loads.append(pltpu.make_async_copy(a_hbm.at[0, 0, s, 0], abuf.at[0, c, rows], load_sem.at[2 * s + 1]))
    for load in loads:
        load.start()

    barrier = pltpu.get_barrier_semaphore()
    pl.semaphore_signal(barrier, inc=1, device_id=sib)
    for n in range(1, n_col):
        pl.semaphore_signal(barrier, inc=1, device_id={"col": lax.rem(c + n, n_col)})

    @pl.when(r > 0)
    def _():
        pl.semaphore_signal(barrier, inc=1, device_id={"row": r - 1})

    @pl.when(r < n_row - 1)
    def _():
        pl.semaphore_signal(barrier, inc=1, device_id={"row": r + 1})

    a_codes, b_codes = [], []
    for s in range(steps):
        a_codes.append(jnp.where(c < ac[0, d, s], ai[0, 0, s, 0], -1))
        pos = bi[0, 0, s, 0]
        b_codes.append(pos // CB)
        b_codes.append(jnp.where(r < bc[0, d, s], pos % CB, -1))
    abuf[0, c, pl.ds(steps * BS, TAIL)] = _rows(a_codes)
    bbuf[0, r, pl.ds(steps * BS, TAIL)] = _rows(b_codes)

    def b_copy(t, sems, target):
        return pltpu.make_async_remote_copy(
            src_ref=bbuf.at[0, t], dst_ref=bbuf.at[0, t], send_sem=sems.at[t], recv_sem=b_recv.at[t],
            device_id={"row": target}, device_id_type=pl.DeviceIdType.MESH)

    def b_across(t):
        return pltpu.make_async_remote_copy(
            src_ref=bbuf.at[0, t], dst_ref=bbuf.at[1, t], send_sem=b_send2.at[t], recv_sem=b_recv2.at[t],
            device_id=sib, device_id_type=pl.DeviceIdType.MESH)

    def a_copy(n, origin, target):
        return pltpu.make_async_remote_copy(
            src_ref=abuf.at[0, origin], dst_ref=abuf.at[0, origin], send_sem=a_send.at[n], recv_sem=a_recv.at[n],
            device_id={"col": target}, device_id_type=pl.DeviceIdType.MESH)

    def a_across(t):
        return pltpu.make_async_remote_copy(
            src_ref=abuf.at[0, t], dst_ref=abuf.at[1, t], send_sem=a_send2.at[t], recv_sem=a_recv2.at[t],
            device_id=sib, device_id_type=pl.DeviceIdType.MESH)

    pl.semaphore_wait(barrier, n_col + jnp.where(r > 0, 1, 0) + jnp.where(r < n_row - 1, 1, 0))
    for load in loads:
        load.wait()

    @pl.when(r < n_row - 1)
    def _():
        b_copy(r, b_right, r + 1).start()

    @pl.when(r > 0)
    def _():
        b_copy(r, b_left, r - 1).start()

    for n in range(n_col - 1, 0, -1):
        a_copy(n, c, c ^ n).start()
    a_across(c).start()
    b_across(r).start()

    def pass_on(gap):
        @pl.when(r >= gap)
        def _():
            t = r - gap
            b_copy(t, b_right, r).wait_recv()

            @pl.when(r < n_row - 1)
            def _():
                b_copy(t, b_right, r + 1).start()

            b_across(t).start()

        @pl.when(r + gap < n_row)
        def _():
            t = r + gap
            b_copy(t, b_left, r).wait_recv()

            @pl.when(r > 0)
            def _():
                b_copy(t, b_left, r - 1).start()

            b_across(t).start()

    def chunk(which, t, first):
        b_tail = bbuf[which, t, pl.ds(steps * BS, TAIL)].astype(F32)
        a_tails = [abuf[which, u, pl.ds(steps * BS, TAIL)].astype(F32) for u in range(n_col)]
        xs, ys = [], []
        for s in range(steps):
            rows = pl.ds(s * BS, BS)
            inner = jnp.broadcast_to(b_tail[2 * s:2 * s + 1], (TAIL, BS))
            column = jnp.broadcast_to(b_tail[2 * s + 1:2 * s + 2], (TAIL, BS))
            codes = [jnp.broadcast_to(tail[s:s + 1], (TAIL, BS)) - inner for tail in a_tails]
            blocks = [abuf[which, u, rows] for u in range(n_col)]
            parts = []
            for i in range(RB):
                total = None
                for u in range(n_col):
                    keep = jnp.where(codes[u] == float(i * PW), 1.0, 0.0).astype(BF)
                    term = _times(keep, blocks[u])
                    total = term if total is None else total + term
                parts.append(total)
            xs.append(jnp.concatenate(parts, axis=0))
            block = bbuf[which, t, rows]
            wanted = column - (d * half).astype(F32)
            ys.append(jnp.concatenate(
                [_times(jnp.where(wanted == float(j), 1.0, 0.0).astype(BF), block) for j in range(half)], axis=1))
        x = jnp.concatenate(xs, axis=1)
        y = jnp.concatenate(ys, axis=0)
        product = jnp.dot(x, y, preferred_element_type=F32)
        if first:
            acc[...] = product
        else:
            acc[...] += product

    pass_on(1)
    for n in range(1, n_col):
        a_copy(n, c, c ^ n).wait_recv()
        a_across(c ^ n).start()
    if n_row > 2:
        pass_on(2)
    chunk(0, r, True)
    chunk(0, r ^ 1, False)
    for gap in range(3, n_row):
        pass_on(gap)
    for n in range(2, n_row):
        chunk(0, r ^ n, False)
    for u in range(n_col):
        a_across(u).wait_recv()
    for n in range(n_row):
        b_across(r ^ n).wait_recv()
        chunk(1, r ^ n, False)

    for i in range(RB):
        for j in range(half):
            keep = cm[i, j].astype(F32)
            box = (pl.ds(i * BS, BS), pl.ds(j * BS, BS))
            out_ref[box] = (acc[box] * keep).astype(BF)

    for n in range(1, n_col):
        a_copy(n, c, c ^ n).wait_send()
    for u in range(n_col):
        a_across(u).wait_send()
    for t in range(n_row):
        b_across(t).wait_send()

        @pl.when((r >= t) & (r < n_row - 1))
        def _():
            b_copy(t, b_right, r).wait_send()

        @pl.when((r <= t) & (r > 0))
        def _():
            b_copy(t, b_left, r).wait_send()


def fused(n_row, n_col, *args):
    a_blocks, b_blocks = args[0], args[3]
    steps = a_blocks.shape[2]
    smem = pl.BlockSpec(memory_space=pltpu.SMEM)
    hbm = pl.BlockSpec(memory_space=pl.ANY)
    rows = steps * BS + TAIL
    dma = pltpu.SemaphoreType.DMA
    return pl.pallas_call(
        functools.partial(kernel, n_row, n_col, steps),
        out_shape=jax.ShapeDtypeStruct((RB * BS, CB // 2 * BS), BF),
        in_specs=[hbm, smem, smem, hbm, smem, smem, smem],
        out_specs=pl.BlockSpec(memory_space=pltpu.VMEM),
        scratch_shapes=[
            pltpu.VMEM((2, n_col, rows, BS), BF),
            pltpu.VMEM((2, n_row, rows, BS), BF),
            pltpu.VMEM((RB * BS, CB // 2 * BS), F32),
            dma((2 * steps,)),
            dma((n_col,)), dma((n_col,)), dma((n_col,)), dma((n_col,)),
            dma((n_row,)), dma((n_row,)), dma((n_row,)), dma((n_row,)), dma((n_row,)),
        ],
        compiler_params=pltpu.CompilerParams(
            collective_id=0, has_side_effects=True, vmem_limit_bytes=32 * 2**20),
    )(*args)


def panel_term(a_blk, a_idx, a_cnt, b_blk, b_idx, b_cnt, col_start, col_count):
    a_slots = a_idx.shape[0]
    b_slots = b_idx.shape[0]
    live_a = jnp.arange(a_slots, dtype=jnp.int32) < a_cnt
    onehot_a = (
        (a_idx[:, None] == jnp.arange(RB * PW, dtype=jnp.int32)[None, :]) & live_a[:, None]
    ).astype(jnp.bfloat16)
    dense = jnp.einsum("sp,sxy->pxy", onehot_a, a_blk, preferred_element_type=jnp.float32).astype(
        jnp.bfloat16
    )
    stacked = dense.reshape(RB, PW, BS, BS).transpose(0, 2, 1, 3).reshape(RB * BS, PW, BS)
    inner_b = b_idx // CB
    column_b = b_idx % CB
    live_b = jnp.arange(b_slots, dtype=jnp.int32) < b_cnt
    picker = (inner_b[:, None] == jnp.arange(PW, dtype=jnp.int32)[None, :]).astype(jnp.bfloat16)
    columns = jnp.einsum("sj,mjk->smk", picker, stacked, preferred_element_type=jnp.float32).astype(
        jnp.bfloat16
    )
    products = jnp.einsum("smk,skl->sml", columns, b_blk, preferred_element_type=jnp.float32)
    placer = (
        (column_b[:, None] - col_start == jnp.arange(col_count, dtype=jnp.int32)[None, :])
        & live_b[:, None]
    ).astype(jnp.float32)
    placed = jnp.einsum(
        "sn,sml->mnl",
        placer,
        products,
        precision=lax.Precision.HIGHEST,
        preferred_element_type=jnp.float32,
    )
    return placed.reshape(RB * BS, col_count * BS)


def apply_mask(total, c_mask):
    half = c_mask.shape[1]
    kept = total.reshape(RB, BS, half, BS) * c_mask.astype(jnp.float32)[:, None, :, None]
    return kept.reshape(RB * BS, half * BS).astype(jnp.bfloat16)


def gathered(a_blocks, a_index, a_count, b_blocks, b_index, b_count, c_mask):
    steps = a_blocks.shape[2]
    group = lax.axis_index("depth")
    total = jnp.zeros((RB * BS, CB * BS), jnp.float32)
    for step in range(steps):
        got_a, got_ai = (
            lax.all_gather(a_blocks[:, :, step : step + 1], "col", axis=3, tiled=True),
            lax.all_gather(a_index[:, :, step : step + 1], "col", axis=3, tiled=True),
        )
        got_b, got_bi = (
            lax.all_gather(b_blocks[:, :, step : step + 1], "row", axis=3, tiled=True),
            lax.all_gather(b_index[:, :, step : step + 1], "row", axis=3, tiled=True),
        )
        total = total + panel_term(
            got_a[0, 0, 0],
            got_ai[0, 0, 0],
            a_count[0, group, step],
            got_b[0, 0, 0],
            got_bi[0, 0, 0],
            b_count[0, group, step],
            0,
            CB,
        )
    summed = lax.psum_scatter(
        total.astype(jnp.bfloat16), "depth", scatter_dimension=1, tiled=True
    ).astype(jnp.float32)
    return apply_mask(summed, c_mask)


def solution(mesh):
    n_row, n_col, n_depth = (mesh.shape[axis] for axis in ("row", "col", "depth"))

    def local(*args):
        one_slot_each = args[0].shape[3] == 1 and args[3].shape[3] == 1
        short = n_depth == 2 and one_slot_each and n_row in (2, 4, 8) and n_col in (2, 4, 8)
        return fused(n_row, n_col, *args) if short else gathered(*args)

    in_specs = (
        P("row", "depth", None, "col", None, None),
        P("row", "depth", None, "col"),
        P("row", None, None),
        P("col", "depth", None, "row", None, None),
        P("col", "depth", None, "row"),
        P("col", None, None),
        P("row", ("col", "depth")),
    )
    out_specs = P("row", ("col", "depth"))
    return jax.shard_map(local, mesh=mesh, in_specs=in_specs, out_specs=out_specs, check_vma=False)
```

```python
import functools

import jax
import jax.numpy as jnp
from jax import lax
from jax.experimental import pallas as pl
from jax.experimental.pallas import tpu as pltpu
from jax.sharding import PartitionSpec as P

BS = 128
PW = 8
RB = 4
CB = 8
TAIL = 16
BF = jnp.bfloat16
F32 = jnp.float32


def _rows(values):
    row = lax.broadcasted_iota(jnp.int32, (TAIL, BS), 0)
    tile = jnp.zeros((TAIL, BS), jnp.int32)
    for r, value in enumerate(values):
        tile = jnp.where(row == r, value, tile)
    return tile.astype(F32).astype(BF)


def _times(mask, block):
    return (block.reshape(BS // TAIL, TAIL, BS) * mask[None]).reshape(BS, BS)


def kernel(n_row, n_col, steps,
           a_hbm, ai_hbm, ac_hbm, b_hbm, bi_hbm, bc_hbm, cm_hbm, out_ref,
           abuf, bbuf, acc, ai, ac, bi, bc, cm,
           load_sem, small_sem, a_send, a_recv, a_send2, a_recv2,
           b_send, b_recv, b_send2, b_recv2):
    r = lax.axis_index("row")
    c = lax.axis_index("col")
    d = lax.axis_index("depth")
    sib = {"depth": 1 - d}
    half = CB // 2

    small = [pltpu.make_async_copy(src, dst, small_sem.at[n]) for n, (src, dst) in enumerate(
        [(ai_hbm, ai), (ac_hbm, ac), (bi_hbm, bi), (bc_hbm, bc), (cm_hbm, cm)])]
    for load in small:
        load.start()
    loads = []
    for s in range(steps):
        rows = pl.ds(TAIL + s * BS, BS)
        loads.append(pltpu.make_async_copy(b_hbm.at[0, 0, s, 0], bbuf.at[0, r, rows], load_sem.at[2 * s]))
        loads.append(pltpu.make_async_copy(a_hbm.at[0, 0, s, 0], abuf.at[0, c, rows], load_sem.at[2 * s + 1]))
    for load in loads:
        load.start()

    barrier = pltpu.get_barrier_semaphore()
    pl.semaphore_signal(barrier, inc=1, device_id=sib)
    for n in range(1, n_col):
        pl.semaphore_signal(barrier, inc=1, device_id={"col": lax.rem(c + n, n_col)})

    for n in range(1, n_row):
        pl.semaphore_signal(barrier, inc=1, device_id={"row": r ^ n})

    for load in small:
        load.wait()
    a_codes, b_codes = [], []
    for s in range(steps):
        a_codes.append(jnp.where(c < ac[d, s], ai[0, s], -1))
        pos = bi[0, s]
        b_codes.append(pos // CB)
        b_codes.append(jnp.where(r < bc[d, s], pos % CB, -1))
    abuf[0, c, pl.ds(0, TAIL)] = _rows(a_codes)
    bbuf[0, r, pl.ds(0, TAIL)] = _rows(b_codes)

    pieces = [pl.ds(0, TAIL + BS)] + [pl.ds(TAIL + s * BS, BS) for s in range(1, steps)]

    def remote(src, dst, send, recv, target):
        return pltpu.make_async_remote_copy(
            src_ref=src, dst_ref=dst, send_sem=send, recv_sem=recv,
            device_id=target, device_id_type=pl.DeviceIdType.MESH)

    def b_copy(n, p, origin, target):
        ref = bbuf.at[0, origin, pieces[p]]
        return remote(ref, ref, b_send.at[n, p], b_recv.at[n, p], {"row": target})

    def b_across(t, p):
        return remote(bbuf.at[0, t, pieces[p]], bbuf.at[1, t, pieces[p]], b_send2.at[t, p], b_recv2.at[t, p], sib)

    def a_copy(n, p, origin, target):
        ref = abuf.at[0, origin, pieces[p]]
        return remote(ref, ref, a_send.at[n, p], a_recv.at[n, p], {"col": target})

    def a_across(t, p):
        return remote(abuf.at[0, t, pieces[p]], abuf.at[1, t, pieces[p]], a_send2.at[t, p], a_recv2.at[t, p], sib)

    pl.semaphore_wait(barrier, n_col + n_row - 1)
    for load in loads:
        load.wait()

    for p in range(steps):
        for n in range(1, n_row):
            b_copy(n, p, r, r ^ n).start()
        for n in range(n_col - 1, 0, -1):
            a_copy(n, p, c, c ^ n).start()
    for p in range(steps):
        b_across(r, p).start()
        a_across(c, p).start()

    def factors(which, t):
        b_tail = bbuf[which, t, pl.ds(0, TAIL)].astype(F32)
        a_tails = [abuf[which, u, pl.ds(0, TAIL)].astype(F32) for u in range(n_col)]
        xs, ys = [], []
        for s in range(steps):
            rows = pl.ds(TAIL + s * BS, BS)
            inner = jnp.broadcast_to(b_tail[2 * s:2 * s + 1], (TAIL, BS))
            column = jnp.broadcast_to(b_tail[2 * s + 1:2 * s + 2], (TAIL, BS))
            codes = [jnp.broadcast_to(tail[s:s + 1], (TAIL, BS)) - inner for tail in a_tails]
            blocks = [abuf[which, u, rows] for u in range(n_col)]
            parts = []
            for i in range(RB):
                total = None
                for u in range(n_col):
                    keep = jnp.where(codes[u] == float(i * PW), 1.0, 0.0).astype(BF)
                    term = _times(keep, blocks[u])
                    total = term if total is None else total + term
                parts.append(total)
            xs.append(jnp.concatenate(parts, axis=0))
            block = bbuf[which, t, rows]
            wanted = column - (d * half).astype(F32)
            ys.append(jnp.concatenate(
                [_times(jnp.where(wanted == float(j), 1.0, 0.0).astype(BF), block) for j in range(half)], axis=1))
        return xs, ys

    def stage(t, first):
        mine, other = factors(0, t), factors(1, t)
        x = jnp.concatenate(mine[0] + other[0], axis=1)
        y = jnp.concatenate(mine[1] + other[1], axis=0)
        product = jnp.dot(x, y, preferred_element_type=F32)
        if first:
            acc[...] = product
        else:
            acc[...] += product

    for p in range(steps):
        for n in range(1, n_col):
            a_copy(n, p, c, c ^ n).wait_recv()
            a_across(c ^ n, p).start()
    for n in range(1, n_row):
        for p in range(steps):
            b_copy(n, p, r, r ^ n).wait_recv()
            b_across(r ^ n, p).start()
    for u in range(n_col):
        for p in range(steps):
            a_across(u, p).wait_recv()
    for n in range(n_row):
        for p in range(steps):
            b_across(r ^ n, p).wait_recv()
        stage(r ^ n, n == 0)

    for i in range(RB):
        for j in range(half):
            keep = cm[i, j].astype(F32)
            box = (pl.ds(i * BS, BS), pl.ds(j * BS, BS))
            out_ref[box] = (acc[box] * keep).astype(BF)

    for p in range(steps):
        for n in range(1, n_col):
            a_copy(n, p, c, c ^ n).wait_send()
        for u in range(n_col):
            a_across(u, p).wait_send()
        for n in range(1, n_row):
            b_copy(n, p, r, r ^ n).wait_send()
        for t in range(n_row):
            b_across(t, p).wait_send()


def fused(n_row, n_col, *args):
    a_blocks, a_index, a_count, b_blocks, b_index, b_count, c_mask = args
    steps = a_blocks.shape[2]
    args = (a_blocks, a_index.reshape(1, steps), a_count.reshape(a_count.shape[1:]),
            b_blocks, b_index.reshape(1, steps), b_count.reshape(b_count.shape[1:]), c_mask)
    hbm = pl.BlockSpec(memory_space=pltpu.HBM)
    rows = steps * BS + TAIL
    dma = pltpu.SemaphoreType.DMA
    return pl.pallas_call(
        functools.partial(kernel, n_row, n_col, steps),
        out_shape=jax.ShapeDtypeStruct((RB * BS, CB // 2 * BS), BF),
        in_specs=[hbm] * 7,
        out_specs=pl.BlockSpec(memory_space=pltpu.VMEM),
        scratch_shapes=[
            pltpu.VMEM((2, n_col, rows, BS), BF),
            pltpu.VMEM((2, n_row, rows, BS), BF),
            pltpu.VMEM((RB * BS, CB // 2 * BS), F32),
            pltpu.SMEM((1, steps), jnp.int32),
            pltpu.SMEM((2, steps), jnp.int32),
            pltpu.SMEM((1, steps), jnp.int32),
            pltpu.SMEM((2, steps), jnp.int32),
            pltpu.SMEM(c_mask.shape, jnp.int32),
            dma((2 * steps,)), dma((5,)),
            dma((n_col, steps)), dma((n_col, steps)), dma((n_col, steps)), dma((n_col, steps)),
            dma((n_row, steps)), dma((n_row, steps)), dma((n_row, steps)), dma((n_row, steps)),
        ],
        compiler_params=pltpu.CompilerParams(
            collective_id=0, has_side_effects=True, vmem_limit_bytes=63 * 2**20),
    )(*args)


def panel_term(a_blk, a_idx, a_cnt, b_blk, b_idx, b_cnt, col_start, col_count):
    a_slots = a_idx.shape[0]
    b_slots = b_idx.shape[0]
    live_a = jnp.arange(a_slots, dtype=jnp.int32) < a_cnt
    onehot_a = (
        (a_idx[:, None] == jnp.arange(RB * PW, dtype=jnp.int32)[None, :]) & live_a[:, None]
    ).astype(jnp.bfloat16)
    dense = jnp.einsum("sp,sxy->pxy", onehot_a, a_blk, preferred_element_type=jnp.float32).astype(
        jnp.bfloat16
    )
    stacked = dense.reshape(RB, PW, BS, BS).transpose(0, 2, 1, 3).reshape(RB * BS, PW, BS)
    inner_b = b_idx // CB
    column_b = b_idx % CB
    live_b = jnp.arange(b_slots, dtype=jnp.int32) < b_cnt
    picker = (inner_b[:, None] == jnp.arange(PW, dtype=jnp.int32)[None, :]).astype(jnp.bfloat16)
    columns = jnp.einsum("sj,mjk->smk", picker, stacked, preferred_element_type=jnp.float32).astype(
        jnp.bfloat16
    )
    products = jnp.einsum("smk,skl->sml", columns, b_blk, preferred_element_type=jnp.float32)
    placer = (
        (column_b[:, None] - col_start == jnp.arange(col_count, dtype=jnp.int32)[None, :])
        & live_b[:, None]
    ).astype(jnp.float32)
    placed = jnp.einsum(
        "sn,sml->mnl",
        placer,
        products,
        precision=lax.Precision.HIGHEST,
        preferred_element_type=jnp.float32,
    )
    return placed.reshape(RB * BS, col_count * BS)


def apply_mask(total, c_mask):
    half = c_mask.shape[1]
    kept = total.reshape(RB, BS, half, BS) * c_mask.astype(jnp.float32)[:, None, :, None]
    return kept.reshape(RB * BS, half * BS).astype(jnp.bfloat16)


def gathered(a_blocks, a_index, a_count, b_blocks, b_index, b_count, c_mask):
    steps = a_blocks.shape[2]
    group = lax.axis_index("depth")
    total = jnp.zeros((RB * BS, CB * BS), jnp.float32)
    for step in range(steps):
        got_a, got_ai = (
            lax.all_gather(a_blocks[:, :, step : step + 1], "col", axis=3, tiled=True),
            lax.all_gather(a_index[:, :, step : step + 1], "col", axis=3, tiled=True),
        )
        got_b, got_bi = (
            lax.all_gather(b_blocks[:, :, step : step + 1], "row", axis=3, tiled=True),
            lax.all_gather(b_index[:, :, step : step + 1], "row", axis=3, tiled=True),
        )
        total = total + panel_term(
            got_a[0, 0, 0],
            got_ai[0, 0, 0],
            a_count[0, group, step],
            got_b[0, 0, 0],
            got_bi[0, 0, 0],
            b_count[0, group, step],
            0,
            CB,
        )
    summed = lax.psum_scatter(
        total.astype(jnp.bfloat16), "depth", scatter_dimension=1, tiled=True
    ).astype(jnp.float32)
    return apply_mask(summed, c_mask)


def solution(mesh):
    n_row, n_col, n_depth = (mesh.shape[axis] for axis in ("row", "col", "depth"))

    def local(*args):
        one_slot_each = args[0].shape[3] == 1 and args[3].shape[3] == 1
        short = n_depth == 2 and one_slot_each and n_row in (2, 4, 8) and n_col in (2, 4, 8)
        return fused(n_row, n_col, *args) if short else gathered(*args)

    in_specs = (
        P("row", "depth", None, "col", None, None),
        P("row", "depth", None, "col"),
        P("row", None, None),
        P("col", "depth", None, "row", None, None),
        P("col", "depth", None, "row"),
        P("col", None, None),
        P("row", ("col", "depth")),
    )
    out_specs = P("row", ("col", "depth"))
    return jax.shard_map(local, mesh=mesh, in_specs=in_specs, out_specs=out_specs, check_vma=False)
```

```python
import functools

import jax
import jax.numpy as jnp
from jax import lax
from jax.experimental import pallas as pl
from jax.experimental.pallas import tpu as pltpu
from jax.sharding import PartitionSpec as P

BS = 128
PW = 8
RB = 4
CB = 8
TAIL = 16
BF = jnp.bfloat16
F32 = jnp.float32


def _rows(values):
    row = lax.broadcasted_iota(jnp.int32, (TAIL, BS), 0)
    tile = jnp.zeros((TAIL, BS), jnp.int32)
    for r, value in enumerate(values):
        tile = jnp.where(row == r, value, tile)
    return tile.astype(F32).astype(BF)


def _times(mask, block):
    return (block.reshape(BS // TAIL, TAIL, BS) * mask[None]).reshape(BS, BS)


def kernel(n_row, n_col, steps,
           a_hbm, ai_hbm, ac_hbm, b_hbm, bi_hbm, bc_hbm, cm_hbm, out_ref,
           abuf, bbuf, acc, ai, ac, bi, bc, cm,
           load_sem, small_sem, a_send, a_recv, a_send2, a_recv2,
           b_send, b_recv, b_send2, b_recv2):
    r = lax.axis_index("row")
    c = lax.axis_index("col")
    d = lax.axis_index("depth")
    sib = {"depth": 1 - d}
    half = CB // 2

    small = [pltpu.make_async_copy(src, dst, small_sem.at[n]) for n, (src, dst) in enumerate(
        [(ai_hbm, ai), (ac_hbm, ac), (bi_hbm, bi), (bc_hbm, bc), (cm_hbm, cm)])]
    for load in small:
        load.start()
    loads = []
    for s in range(steps):
        rows = pl.ds(TAIL + s * BS, BS)
        loads.append(pltpu.make_async_copy(b_hbm.at[0, 0, s, 0], bbuf.at[0, r, rows], load_sem.at[2 * s]))
        loads.append(pltpu.make_async_copy(a_hbm.at[0, 0, s, 0], abuf.at[0, c, rows], load_sem.at[2 * s + 1]))
    for load in loads:
        load.start()

    barrier = pltpu.get_barrier_semaphore()
    pl.semaphore_signal(barrier, inc=1, device_id=sib)
    for n in range(1, n_col):
        pl.semaphore_signal(barrier, inc=1, device_id={"col": lax.rem(c + n, n_col)})

    for n in range(1, n_row):
        pl.semaphore_signal(barrier, inc=1, device_id={"row": r ^ n})

    for load in small:
        load.wait()
    a_codes, b_codes = [], []
    for s in range(steps):
        a_codes.append(jnp.where(c < ac[d, s], ai[0, s], -1))
        pos = bi[0, s]
        b_codes.append(pos // CB)
        b_codes.append(jnp.where(r < bc[d, s], pos % CB, -1))
    abuf[0, c, pl.ds(0, TAIL)] = _rows(a_codes)
    bbuf[0, r, pl.ds(0, TAIL)] = _rows(b_codes)

    pieces = [pl.ds(0, TAIL + BS)] + [pl.ds(TAIL + s * BS, BS) for s in range(1, steps)]

    def remote(src, dst, send, recv, target):
        return pltpu.make_async_remote_copy(
            src_ref=src, dst_ref=dst, send_sem=send, recv_sem=recv,
            device_id=target, device_id_type=pl.DeviceIdType.MESH)

    def b_copy(n, p, origin, target):
        ref = bbuf.at[0, origin, pieces[p]]
        return remote(ref, ref, b_send.at[n, p], b_recv.at[n, p], {"row": target})

    def b_across(t, p):
        return remote(bbuf.at[0, t, pieces[p]], bbuf.at[1, t, pieces[p]], b_send2.at[t, p], b_recv2.at[t, p], sib)

    def a_copy(n, p, origin, target):
        ref = abuf.at[0, origin, pieces[p]]
        return remote(ref, ref, a_send.at[n, p], a_recv.at[n, p], {"col": target})

    def a_across(t, p):
        return remote(abuf.at[0, t, pieces[p]], abuf.at[1, t, pieces[p]], a_send2.at[t, p], a_recv2.at[t, p], sib)

    pl.semaphore_wait(barrier, n_col + n_row - 1)
    for load in loads:
        load.wait()

    for p in range(steps):
        for n in range(1, n_row):
            b_copy(n, p, r, r ^ n).start()
        for n in range(n_col - 1, 0, -1):
            a_copy(n, p, c, c ^ n).start()
    for p in range(steps):
        b_across(r, p).start()
        a_across(c, p).start()

    def factors(which, t):
        b_tail = bbuf[which, t, pl.ds(0, TAIL)].astype(F32)
        a_tails = [abuf[which, u, pl.ds(0, TAIL)].astype(F32) for u in range(n_col)]
        xs, ys = [], []
        for s in range(steps):
            rows = pl.ds(TAIL + s * BS, BS)
            inner = jnp.broadcast_to(b_tail[2 * s:2 * s + 1], (TAIL, BS))
            column = jnp.broadcast_to(b_tail[2 * s + 1:2 * s + 2], (TAIL, BS))
            codes = [jnp.broadcast_to(tail[s:s + 1], (TAIL, BS)) - inner for tail in a_tails]
            blocks = [abuf[which, u, rows] for u in range(n_col)]
            parts = []
            for i in range(RB):
                total = None
                for u in range(n_col):
                    keep = jnp.where(codes[u] == float(i * PW), 1.0, 0.0).astype(BF)
                    term = _times(keep, blocks[u])
                    total = term if total is None else total + term
                parts.append(total)
            xs.append(jnp.concatenate(parts, axis=0))
            block = bbuf[which, t, rows]
            wanted = column - (d * half).astype(F32)
            ys.append(jnp.concatenate(
                [_times(jnp.where(wanted == float(j), 1.0, 0.0).astype(BF), block) for j in range(half)], axis=1))
        return xs, ys

    def stage(t, first):
        mine, other = factors(0, t), factors(1, t)
        x = jnp.concatenate(mine[0] + other[0], axis=1)
        y = jnp.concatenate(mine[1] + other[1], axis=0)
        product = jnp.dot(x, y, preferred_element_type=F32)
        if first:
            acc[...] = product
        else:
            acc[...] += product

    for p in range(steps):
        for n in range(1, n_col):
            a_copy(n, p, c, c ^ n).wait_recv()
            a_across(c ^ n, p).start()
    for n in range(1, n_row):
        for p in range(steps):
            b_copy(n, p, r, r ^ n).wait_recv()
            b_across(r ^ n, p).start()
    for u in range(n_col):
        for p in range(steps):
            a_across(u, p).wait_recv()
    for n in range(n_row):
        for p in range(steps):
            b_across(r ^ n, p).wait_recv()
        stage(r ^ n, n == 0)

    for i in range(RB):
        for j in range(half):
            keep = cm[i, j].astype(F32)
            box = (pl.ds(i * BS, BS), pl.ds(j * BS, BS))
            out_ref[box] = (acc[box] * keep).astype(BF)

    for p in range(steps):
        for n in range(1, n_col):
            a_copy(n, p, c, c ^ n).wait_send()
        for u in range(n_col):
            a_across(u, p).wait_send()
        for n in range(1, n_row):
            b_copy(n, p, r, r ^ n).wait_send()
        for t in range(n_row):
            b_across(t, p).wait_send()


def fused(n_row, n_col, *args):
    a_blocks, a_index, a_count, b_blocks, b_index, b_count, c_mask = args
    steps = a_blocks.shape[2]
    args = (a_blocks, a_index.reshape(1, steps), a_count.reshape(a_count.shape[1:]),
            b_blocks, b_index.reshape(1, steps), b_count.reshape(b_count.shape[1:]), c_mask)
    args = tuple(pltpu.with_memory_space_constraint(arg, pltpu.HBM) for arg in args)
    hbm = pl.BlockSpec(memory_space=pltpu.HBM)
    rows = steps * BS + TAIL
    dma = pltpu.SemaphoreType.DMA
    return pl.pallas_call(
        functools.partial(kernel, n_row, n_col, steps),
        out_shape=jax.ShapeDtypeStruct((RB * BS, CB // 2 * BS), BF),
        in_specs=[hbm] * 7,
        out_specs=pl.BlockSpec(memory_space=pltpu.VMEM),
        scratch_shapes=[
            pltpu.VMEM((2, n_col, rows, BS), BF),
            pltpu.VMEM((2, n_row, rows, BS), BF),
            pltpu.VMEM((RB * BS, CB // 2 * BS), F32),
            pltpu.SMEM((1, steps), jnp.int32),
            pltpu.SMEM((2, steps), jnp.int32),
            pltpu.SMEM((1, steps), jnp.int32),
            pltpu.SMEM((2, steps), jnp.int32),
            pltpu.SMEM(c_mask.shape, jnp.int32),
            dma((2 * steps,)), dma((5,)),
            dma((n_col, steps)), dma((n_col, steps)), dma((n_col, steps)), dma((n_col, steps)),
            dma((n_row, steps)), dma((n_row, steps)), dma((n_row, steps)), dma((n_row, steps)),
        ],
        compiler_params=pltpu.CompilerParams(
            collective_id=0, has_side_effects=True, vmem_limit_bytes=32 * 2**20),
    )(*args)


def panel_term(a_blk, a_idx, a_cnt, b_blk, b_idx, b_cnt, col_start, col_count):
    a_slots = a_idx.shape[0]
    b_slots = b_idx.shape[0]
    live_a = jnp.arange(a_slots, dtype=jnp.int32) < a_cnt
    onehot_a = (
        (a_idx[:, None] == jnp.arange(RB * PW, dtype=jnp.int32)[None, :]) & live_a[:, None]
    ).astype(jnp.bfloat16)
    dense = jnp.einsum("sp,sxy->pxy", onehot_a, a_blk, preferred_element_type=jnp.float32).astype(
        jnp.bfloat16
    )
    stacked = dense.reshape(RB, PW, BS, BS).transpose(0, 2, 1, 3).reshape(RB * BS, PW, BS)
    inner_b = b_idx // CB
    column_b = b_idx % CB
    live_b = jnp.arange(b_slots, dtype=jnp.int32) < b_cnt
    picker = (inner_b[:, None] == jnp.arange(PW, dtype=jnp.int32)[None, :]).astype(jnp.bfloat16)
    columns = jnp.einsum("sj,mjk->smk", picker, stacked, preferred_element_type=jnp.float32).astype(
        jnp.bfloat16
    )
    products = jnp.einsum("smk,skl->sml", columns, b_blk, preferred_element_type=jnp.float32)
    placer = (
        (column_b[:, None] - col_start == jnp.arange(col_count, dtype=jnp.int32)[None, :])
        & live_b[:, None]
    ).astype(jnp.float32)
    placed = jnp.einsum(
        "sn,sml->mnl",
        placer,
        products,
        precision=lax.Precision.HIGHEST,
        preferred_element_type=jnp.float32,
    )
    return placed.reshape(RB * BS, col_count * BS)


def apply_mask(total, c_mask):
    half = c_mask.shape[1]
    kept = total.reshape(RB, BS, half, BS) * c_mask.astype(jnp.float32)[:, None, :, None]
    return kept.reshape(RB * BS, half * BS).astype(jnp.bfloat16)


def gathered(a_blocks, a_index, a_count, b_blocks, b_index, b_count, c_mask):
    steps = a_blocks.shape[2]
    group = lax.axis_index("depth")
    total = jnp.zeros((RB * BS, CB * BS), jnp.float32)
    for step in range(steps):
        got_a, got_ai = (
            lax.all_gather(a_blocks[:, :, step : step + 1], "col", axis=3, tiled=True),
            lax.all_gather(a_index[:, :, step : step + 1], "col", axis=3, tiled=True),
        )
        got_b, got_bi = (
            lax.all_gather(b_blocks[:, :, step : step + 1], "row", axis=3, tiled=True),
            lax.all_gather(b_index[:, :, step : step + 1], "row", axis=3, tiled=True),
        )
        total = total + panel_term(
            got_a[0, 0, 0],
            got_ai[0, 0, 0],
            a_count[0, group, step],
            got_b[0, 0, 0],
            got_bi[0, 0, 0],
            b_count[0, group, step],
            0,
            CB,
        )
    summed = lax.psum_scatter(
        total.astype(jnp.bfloat16), "depth", scatter_dimension=1, tiled=True
    ).astype(jnp.float32)
    return apply_mask(summed, c_mask)


def solution(mesh):
    n_row, n_col, n_depth = (mesh.shape[axis] for axis in ("row", "col", "depth"))

    def local(*args):
        one_slot_each = args[0].shape[3] == 1 and args[3].shape[3] == 1
        short = n_depth == 2 and one_slot_each and n_row in (2, 4, 8) and n_col in (2, 4, 8)
        return fused(n_row, n_col, *args) if short else gathered(*args)

    in_specs = (
        P("row", "depth", None, "col", None, None),
        P("row", "depth", None, "col"),
        P("row", None, None),
        P("col", "depth", None, "row", None, None),
        P("col", "depth", None, "row"),
        P("col", None, None),
        P("row", ("col", "depth")),
    )
    out_specs = P("row", ("col", "depth"))
    return jax.shard_map(local, mesh=mesh, in_specs=in_specs, out_specs=out_specs, check_vma=False)
```
